32 devices in a mesh: groups: 2 (over x), gx: 16 (over z, y, core).
Axes of the slice: x: 2, y: 2, z: 4, core: 2. Of those that a mesh axis runs over, the one named last changes fastest.
Arguments:
- inputs: bfloat16 [16, 256, 6144], P('gx', 'groups'), parts along dimension 1, may hold values from -6 to 6
- weight: bfloat16 [16, 12288, 3072], P('gx', 'groups'), parts along dimension 1, may hold values from -0.0546875 to 0.0546875
- preact: bfloat16 [16, 1024, 3072], P('gx', 'groups'), parts along dimension 1, may hold values from -6 to 6
- out_grad: bfloat16 [16, 1024, 3072], P('gx', 'groups'), parts along dimension 1, may hold values from -4 to 4
Outputs:
- in_grad: bfloat16 [16, 256, 6144], P('gx', 'groups'), parts along dimension 1
- weight_grad: bfloat16 [16, 12288, 3072], P('gx', 'groups'), parts along dimension 1
The draws below stay inside these ranges and needn't reach their ends.
There are 2 independent parts, one for each index of `groups`. The reference program is written for one: setup_inputs(seed, part) draws one part's arguments, and reference() takes and returns one part's arrays. A program takes and returns all parts, laid end to end along the dimension named above; each array names one. Nothing has to cross between parts.
All inputs are finite; a program needn't handle non-finite values.
Results may differ from the reference program's by a relative error of at most 0.0049.
Values may be sent and summed in bfloat16 or wider, within the bound.
A program may use at most 256 MiB of HBM per device.

```python
import math
import jax
import jax.numpy as jnp

D = 12288
FF = 24576
TOKENS = 1024
GC = 8
GR = 2
DB = 6144
FB = 3072
TR = 512
TC = 128
N_GX = 16


def level_of(rng, dims, shards, smallest, largest):
    level, own = 1.0, jax.random.fold_in(rng, 6)
    for dim, blocks in shards:
        heights = jnp.exp(jax.random.uniform(jax.random.fold_in(own, dim), (blocks,), jnp.float32, smallest / len(shards), largest / len(shards)))
        level = level * jnp.repeat(heights, dims[dim] // blocks).reshape([-1 if axis == dim else 1 for axis in range(len(dims))])
    return level


def centred(stream_key, extent, spread, limit, split=(), kind=jnp.bfloat16):
    entries = spread * jax.random.normal(stream_key, extent, jnp.float32)
    if split:
        entries = entries * level_of(stream_key, extent, split, -0.22, 0.18)
    return jnp.clip(entries, -limit, limit).astype(kind)


def setup_inputs(seed: int = 0, part: int = 0) -> dict:
    splits = jax.random.split(jax.random.key(seed), 5)
    own_keys = jax.random.split(jax.random.fold_in(splits[4], part), 5)
    inputs = centred(own_keys[0], (N_GX, TC, DB), 1.0, 6.0, ((0, 16),))
    weight = centred(own_keys[1], (N_GX, DB, FB), D ** -0.5, 0.0546875, ((0, 16),))
    preact = centred(own_keys[2], (N_GX, TR, FB), 1.5, 6.0, ((0, 16),))
    out_grad = centred(own_keys[3], (N_GX, TR, FB), 0.25, 4.0, ((0, 16),))
    return dict(inputs=inputs, weight=weight, preact=preact, out_grad=out_grad)


def gelu_slope(gradient, preact):
    value = preact.astype(jnp.float32)
    coeff = math.sqrt(2.0 / math.pi)
    inner = coeff * (value + 0.044715 * value * value * value)
    tangent = jnp.tanh(inner)
    slope = 0.5 * (1.0 + tangent) + 0.5 * value * (1.0 - tangent * tangent) * coeff * (1.0 + 3.0 * 0.044715 * value * value)
    return (gradient.astype(jnp.float32) * slope).astype(jnp.bfloat16)

def reference(inputs, weight, preact, out_grad):
    x_full = inputs.reshape(GR, GC, TC, DB).transpose(1, 2, 0, 3).reshape(TOKENS, D)
    w_full = weight.reshape(GR, GC, DB, FB).transpose(0, 2, 1, 3).reshape(D, FF)
    p_full = preact.reshape(GR, GC, TR, FB).transpose(0, 2, 1, 3).reshape(TOKENS, FF)
    g_full = out_grad.reshape(GR, GC, TR, FB).transpose(0, 2, 1, 3).reshape(TOKENS, FF)
    dy_full = gelu_slope(g_full, p_full)
    dx_full = jnp.dot(dy_full, w_full.T, preferred_element_type=jnp.float32).astype(jnp.bfloat16)
    dw_full = jnp.dot(x_full.T, dy_full, preferred_element_type=jnp.float32).astype(jnp.bfloat16)
    in_grad = dx_full.reshape(GC, TC, GR, DB).transpose(2, 0, 1, 3).reshape(GR * GC, TC, DB)
    weight_grad = dw_full.reshape(GR, DB, GC, FB).transpose(0, 2, 1, 3).reshape(GR * GC, DB, FB)
    return (in_grad, weight_grad)
```

```python
import math

import jax
import jax.numpy as jnp
from jax import lax
from jax.sharding import PartitionSpec as P

GC = 8
CHUNKS = 4
F32 = jnp.float32
BF16 = jnp.bfloat16


def gelu_slope(gradient, preact):
    value = preact.astype(F32)
    coeff = math.sqrt(2.0 / math.pi)
    inner = coeff * (value + 0.044715 * value * value * value)
    tangent = jnp.tanh(inner)
    slope = 0.5 * (1.0 + tangent) + 0.5 * value * (1.0 - tangent * tangent) * coeff * (
        1.0 + 3.0 * 0.044715 * value * value
    )
    return (gradient.astype(F32) * slope).astype(BF16)


def swap(array, distance):
    size = lax.axis_size("gx")
    return lax.ppermute(array, "gx", [(i, i ^ distance) for i in range(size)])


def join(bit, own, other, axis):
    low = jnp.where(bit == 0, own, other)
    high = jnp.where(bit == 0, other, own)
    return jnp.concatenate([low, high], axis)


def times_wt(rows, w):
    return lax.dot_general(rows, w, (((1,), (1,)), ((), ())), preferred_element_type=F32)


def xt_times(x, dy):
    return lax.dot_general(x, dy, (((0,), (0,)), ((), ())), preferred_element_type=F32)


def take(array, index, axis):
    return lax.dynamic_index_in_dim(array, index, axis, keepdims=False)


def general(index, x, w, preact, out_grad):
    size = lax.axis_size("gx")
    dy = gelu_slope(out_grad, preact)
    distance = GC
    while distance < size:
        dy = join(index // distance % 2, dy, swap(dy, distance), 0)
        distance *= 2
    x_all = x[None]
    for distance in (4, 2, 1):
        bit = index // distance % 2
        x_all = join(bit, x_all, swap(x_all, distance), 0)
    tokens, width = x.shape
    x_all = x_all.reshape(2, 2, 2, tokens, width).transpose(2, 1, 0, 3, 4).reshape(-1, width)
    weight_grad = xt_times(x_all, dy).astype(BF16)
    part = times_wt(dy, w).reshape(2, 2, 2, tokens, -1)
    for distance, axis in ((1, 2), (2, 1), (4, 0)):
        bit = index // distance % 2
        kept = take(part, bit, axis)
        sent = take(part, 1 - bit, axis).astype(BF16)
        part = kept + swap(sent, distance).astype(F32)
    return part.astype(BF16), weight_grad


def two_rows(index, x, w, preact, out_grad):
    row, z, y, core = index // GC, index // 4 % 2, index // 2 % 2, index % 2
    tokens, width = x.shape
    hidden = w.shape[1]
    step = tokens // CHUNKS
    mine = z == row

    g4, p4 = out_grad.reshape(4, tokens, hidden), preact.reshape(4, tokens, hidden)
    dy_own, dy_other = [], []
    for q in range(CHUNKS):
        part = slice(q * step, (q + 1) * step)
        dy_own.append(gelu_slope(g4[:, part], p4[:, part]).reshape(4 * step, hidden))
        dy_other.append(swap(dy_own[-1], GC))

    partner = swap(x, 4)
    x_own, x_other = jnp.where(mine, x, partner), jnp.where(mine, partner, x)

    def spread(piece):
        piece = join(y, piece[None], swap(piece, 2)[None], 0)
        piece = join(core, piece[:, None], swap(piece, 1)[:, None], 1)
        return piece.reshape(4 * tokens, width)

    def order(chunks):
        return jnp.concatenate([c.reshape(4, step, hidden) for c in chunks], 1).reshape(
            4 * tokens, hidden
        )

    def reduce(part):
        part = part.reshape(2, 2, -1, part.shape[-1])
        part = take(part, core, 1).astype(F32) + swap(take(part, 1 - core, 1), 1).astype(F32)
        sent = take(part, 1 - y, 0).astype(BF16)
        return take(part, y, 0) + swap(sent, 2).astype(F32)

    size = lax.axis_size("gx")
    to_own = [(i, i ^ 4) for i in range(size) if i // 4 % 2 != i // GC]
    to_other = [(i, i ^ 4) for i in range(size) if i // 4 % 2 == i // GC]

    def last(piece, pairs):
        return piece, lax.ppermute(piece.astype(BF16), "gx", pairs)

    own_rows = order(dy_own)
    half = width // 2
    own_sum, own_recv = [], []
    for h in range(2):
        part = times_wt(own_rows, w[h * half : (h + 1) * half]).astype(BF16)
        kept, recv = last(reduce(part), to_own)
        own_sum.append(kept)
        own_recv.append(recv)
    own_sum, own_recv = jnp.concatenate(own_sum, 1), jnp.concatenate(own_recv, 1)

    dw_own = xt_times(spread(x_own), own_rows).astype(BF16)

    outs = []
    for q in range(CHUNKS):
        kept, recv = last(reduce(times_wt(dy_other[q], w).astype(BF16)), to_other)
        part = slice(q * step, (q + 1) * step)
        outs.append(
            jnp.where(
                mine,
                own_sum[part] + own_recv[part].astype(F32),
                kept + recv.astype(F32),
            ).astype(BF16)
        )
    weight_grad = (dw_own.astype(F32) + xt_times(spread(x_other), order(dy_other))).astype(BF16)
    return jnp.concatenate(outs, 0), weight_grad


def on_device(inputs, weight, preact, out_grad):
    index = lax.axis_index("gx")
    run = two_rows if lax.axis_size("gx") == 2 * GC else general
    in_grad, weight_grad = run(index, inputs[0], weight[0], preact[0], out_grad[0])
    return in_grad[None], weight_grad[None]


def solution(mesh):
    spec = P("gx", "groups", None)
    return jax.shard_map(
        on_device,
        mesh=mesh,
        in_specs=(spec,) * 4,
        out_specs=(spec, spec),
        check_vma=False,
    )
```

```python
import math

import jax
import jax.numpy as jnp
from jax import lax
from jax.sharding import PartitionSpec as P

GC = 8
PIECES = (6, 4, 4, 2)
GROUPS = ((0, 1), (2, 3))
F32 = jnp.float32
BF16 = jnp.bfloat16


def gelu_slope(gradient, preact):
    value = preact.astype(F32)
    coeff = math.sqrt(2.0 / math.pi)
    inner = coeff * (value + 0.044715 * value * value * value)
    tangent = jnp.tanh(inner)
    slope = 0.5 * (1.0 + tangent) + 0.5 * value * (1.0 - tangent * tangent) * coeff * (
        1.0 + 3.0 * 0.044715 * value * value
    )
    return (gradient.astype(F32) * slope).astype(BF16)


def swap(array, distance):
    size = lax.axis_size("gx")
    return lax.ppermute(array, "gx", [(i, i ^ distance) for i in range(size)])


def join(bit, own, other, axis):
    low = jnp.where(bit == 0, own, other)
    high = jnp.where(bit == 0, other, own)
    return jnp.concatenate([low, high], axis)


def times_wt(rows, w):
    return lax.dot_general(rows, w, (((1,), (1,)), ((), ())), preferred_element_type=F32)


def xt_times(x, dy):
    return lax.dot_general(x, dy, (((0,), (0,)), ((), ())), preferred_element_type=F32)


def take(array, index, axis):
    return lax.dynamic_index_in_dim(array, index, axis, keepdims=False)


def general(index, x, w, preact, out_grad):
    size = lax.axis_size("gx")
    dy = gelu_slope(out_grad, preact)
    distance = GC
    while distance < size:
        dy = join(index // distance % 2, dy, swap(dy, distance), 0)
        distance *= 2
    x_all = x[None]
    for distance in (4, 2, 1):
        bit = index // distance % 2
        x_all = join(bit, x_all, swap(x_all, distance), 0)
    tokens, width = x.shape
    x_all = x_all.reshape(2, 2, 2, tokens, width).transpose(2, 1, 0, 3, 4).reshape(-1, width)
    weight_grad = xt_times(x_all, dy).astype(BF16)
    part = times_wt(dy, w).reshape(2, 2, 2, tokens, -1)
    for distance, axis in ((1, 2), (2, 1), (4, 0)):
        bit = index // distance % 2
        kept = take(part, bit, axis)
        sent = take(part, 1 - bit, axis).astype(BF16)
        part = kept + swap(sent, distance).astype(F32)
    return part.astype(BF16), weight_grad


def after(array, *others):
    return lax.optimization_barrier((array, *others))[0]


def two_rows(index, x, w, preact, out_grad):
    row, z, y, core = index // GC, index // 4 % 2, index // 2 % 2, index % 2
    tokens, width = x.shape
    hidden = w.shape[1]
    unit = tokens // sum(PIECES)
    mine = z == row
    size = lax.axis_size("gx")
    to_own = [(i, i ^ 4) for i in range(size) if i // 4 % 2 != i // GC]
    to_other = [(i, i ^ 4) for i in range(size) if i // 4 % 2 == i // GC]

    def order(pieces):
        pieces = [piece.reshape(4, -1, hidden) for piece in pieces]
        return jnp.concatenate(pieces, 1).reshape(-1, hidden)

    def reduce_core(part):
        part = part.reshape(2, 2, -1, part.shape[-1])
        return take(part, core, 1).astype(F32) + swap(take(part, 1 - core, 1), 1).astype(F32)

    def reduce_y(part, *others):
        received = swap(take(part, 1 - y, 0).astype(BF16), 2)
        return take(part, y, 0) + after(received, *others).astype(F32)

    def last(piece, pairs):
        return lax.ppermute(piece.astype(BF16), "gx", pairs)

    top, bottom = x[: tokens // 2], x[tokens // 2 :]
    top_z, top_y = swap(top, 4), swap(top, 2)
    own_rows = after(gelu_slope(out_grad, preact))
    split = own_rows.reshape(4, tokens, hidden)
    dy = []

    def send_piece(*others):
        low, high = (sum(PIECES[: len(dy) + more]) * unit for more in (0, 1))
        sent = split[:, low:high].reshape(-1, hidden)
        dy.append(swap(after(sent, *dy[-1:], *others), GC))

    send_piece()

    own_rows, top_z, top_y, bottom = lax.optimization_barrier((own_rows, top_z, top_y, bottom))
    bottom_z, bottom_y = swap(bottom, 4), swap(bottom, 2)
    own = times_wt(own_rows, w).astype(BF16)
    own, bottom_z, bottom_y, dy[0] = lax.optimization_barrier((own, bottom_z, bottom_y, dy[0]))
    send_piece()
    x_z = jnp.concatenate([top_z, bottom_z], 0)
    x_y = jnp.concatenate([top_y, bottom_y], 0)
    x_zy = swap(x_z, 2)
    own_core = reduce_core(own)

    dy[1], x_zy, own_core = lax.optimization_barrier((dy[1], x_zy, own_core))
    send_piece()

    def finish(near, far):
        piece = join(y, near[None], far[None], 0)
        piece = join(core, piece[:, None], swap(piece, 1)[:, None], 1)
        return piece.reshape(4 * tokens, width)

    def partial_of(group, *others):
        rows = after(order([dy[q] for q in group]), *others)
        return times_wt(rows, w).astype(BF16)

    own_x = finish(jnp.where(mine, x, x_z), jnp.where(mine, x_y, x_zy))
    rest_x = finish(jnp.where(mine, x_z, x), jnp.where(mine, x_zy, x_y))
    other, dy[2] = lax.optimization_barrier((partial_of(GROUPS[0]), dy[2]))
    send_piece()
    own_sum = reduce_y(own_core, other)
    core_sum = [reduce_core(other)]
    own_x = after(own_x, core_sum[0], own_sum)
    dw_own = xt_times(own_x, own_rows).astype(BF16)
    kept = [reduce_y(core_sum[0], dw_own)]
    core_sum.append(reduce_core(partial_of(GROUPS[1], dw_own, rest_x, kept[0])))
    own_recv, recv = last(own_sum, to_own), [last(kept[0], to_other)]

    all_other = after(order(dy), core_sum[1])
    weight_grad = (dw_own.astype(F32) + xt_times(rest_x, all_other)).astype(BF16)
    kept.append(reduce_y(core_sum[1], weight_grad))
    recv.append(last(kept[1], to_other))
    own_recv, weight_grad, recv[0] = lax.optimization_barrier((own_recv, weight_grad, recv[0]))
    outs, start = [], 0
    for q in range(len(GROUPS)):
        part = slice(start, start + kept[q].shape[0])
        start = part.stop
        outs.append(
            jnp.where(
                mine,
                own_sum[part] + own_recv[part].astype(F32),
                kept[q] + recv[q].astype(F32),
            ).astype(BF16)
        )
    return jnp.concatenate(outs, 0), weight_grad


def on_device(inputs, weight, preact, out_grad):
    index = lax.axis_index("gx")
    run = two_rows if lax.axis_size("gx") == 2 * GC else general
    in_grad, weight_grad = run(index, inputs[0], weight[0], preact[0], out_grad[0])
    return in_grad[None], weight_grad[None]


def solution(mesh):
    spec = P("gx", "groups", None)
    return jax.shard_map(
        on_device,
        mesh=mesh,
        in_specs=(spec,) * 4,
        out_specs=(spec, spec),
        check_vma=False,
    )
```
